512 devices in a mesh: row: 16 (over x, y_hi), col: 32 (over y_lo, z, core).
Axes of the slice: x: 4, y: 8 (y_hi: 4, y_lo: 2; y = y_hi * 2 + y_lo), z: 8, core: 2. Of those that a mesh axis runs over, the one named last changes fastest.
Arguments:
- activations: bfloat16 [2048, 57344], P(('row', 'col')), as said below
Outputs:
- correlation: bfloat16 [8192, 57344], P('row', 'col')
Inputs may be any that keep to these rules, and one draw needn't show every extreme that they name: `activations`: finite values; each unit has a spread of order one or more over the tokens.
All inputs are finite; a program needn't handle non-finite values.
Results may differ from the reference program's by a relative error of at most 0.0039.
Values may be sent and summed in bfloat16 or wider, within the bound.
No kernel may reach another device: no remote copies, remote signals or barrier semaphores. Data moves between devices by JAX's collectives and lax.ppermute only.
A program may use at most 64 MiB of HBM per device.

```python
import jax
import jax.numpy as jnp
from jax import lax

FF = 28672
ROWS_DEV = 512
UNITS = 57344
TOKENS = 2048
N_ROW = 16


def draw_activations(key, part):
    key = jax.random.fold_in(key, 11)
    keys = jax.random.split(key, 7)
    groups = 16
    factor = jax.random.normal(keys[0], (TOKENS, groups), jnp.float32)
    which = jax.random.randint(keys[1], (UNITS,), 0, groups)
    shared = jnp.take(factor, which, axis=1)
    noise_a = jax.random.normal(keys[2], (TOKENS, FF), jnp.float32)
    noise_b = jax.random.normal(keys[3], (TOKENS, FF), jnp.float32)
    top_scale = 10.0
    offset_scale = 2.0
    model_a = 0.6 * shared[:, :FF] + 0.8 * noise_a
    order = jax.random.permutation(keys[4], FF)
    model_b = 0.8 * jnp.take(model_a, order, axis=1) + 0.6 * noise_b
    base = jnp.concatenate([model_a, model_b], axis=1)
    token_scale = 1.0 + 2.0 * jnp.arange(TOKENS, dtype=jnp.float32) / TOKENS
    unit_scale = jnp.exp(jax.random.uniform(keys[5], (UNITS,), jnp.float32, 0.0, jnp.log(top_scale)))
    offset = offset_scale * jax.random.normal(keys[6], (UNITS,), jnp.float32)
    values = (base * token_scale[:, None] + offset[None, :]) * unit_scale[None, :]
    return values.astype(jnp.bfloat16)


def setup_inputs(seed: int = 0) -> dict:
    streams_of = jax.random.split(jax.random.key(seed), 2)
    return {
        "activations": draw_activations(jax.random.fold_in(streams_of[1], 71), 0),
    }


EPS = 1e-06

def standardize(activations):
    values = activations.astype(jnp.float32)
    mean = lax.optimization_barrier(jnp.mean(values, axis=0))
    centered = values - mean
    spread = jnp.sqrt(lax.optimization_barrier(jnp.mean(centered * centered, axis=0)) + EPS)
    return (centered / spread).astype(jnp.bfloat16)

def reference(activations):
    standard = standardize(activations)
    widened = lax.optimization_barrier(standard).astype(jnp.float32)
    slab = ROWS_DEV * N_ROW
    blocks = widened[:, :slab].reshape(TOKENS, N_ROW, ROWS_DEV).transpose(1, 0, 2)

    def one_block(block):
        total = jnp.dot(block.T, widened, precision=lax.Precision.HIGHEST, preferred_element_type=jnp.float32)
        return (total / TOKENS).astype(jnp.bfloat16)
    result = lax.map(one_block, blocks)
    return result.reshape(slab, UNITS)
```

```python
import jax
import jax.numpy as jnp
from jax import lax
from jax.experimental import pallas as pl
from jax.experimental.pallas import tpu as pltpu
from jax.sharding import Mesh, PartitionSpec as P

ROWS_DEV = 512
EPS = 1e-06
TOKENS = 2048
FIRST = 1280
PIECE = 128
TILE = 256


def pairs(core_first):
    perm = []
    for i in range(4):
        for core in range(2):
            flip = core_first if core == 0 else 4 - core_first
            perm.append((i * 2 + core, (i ^ flip) * 2 + core))
    return perm


def exchange(values, axis, step):
    return lax.ppermute(values, (axis, "c"), pairs(1 if step == 0 else 3))


def slab_kernel(order_ref, slab_ref, out_ref, wide, piece):
    n = TOKENS // PIECE
    for block in range(ROWS_DEV // 128):
        lanes = slice(block * 128, (block + 1) * 128)

        def widen(i, total):
            rows = pl.ds(pl.multiple_of(i * PIECE, PIECE), PIECE)
            values = slab_ref[rows, lanes].astype(jnp.float32)
            wide[block, rows, :] = values
            return total + jnp.sum(values.reshape(PIECE // 8, 8, 128), axis=0)

        def square(i, total):
            centered = wide[block, pl.ds(pl.multiple_of(i * PIECE, PIECE), PIECE), :] - mean
            return total + jnp.sum((centered * centered).reshape(PIECE // 8, 8, 128), axis=0)

        zero = jnp.zeros((8, 128), jnp.float32)
        mean = jnp.sum(lax.fori_loop(0, n, widen, zero), axis=0, keepdims=True) / TOKENS
        variance = jnp.sum(lax.fori_loop(0, n, square, zero), axis=0, keepdims=True) / TOKENS
        scale = 1.0 / jnp.sqrt(variance + EPS)
        for slot in range(n):
            first = order_ref[slot] * 8
            for half in range(2):
                for token in range(4):
                    rows = wide[block, pl.ds(first + half * 4 + token, 16, stride=128), :]
                    piece[pl.ds(half * 64 + token, 16, stride=4), :] = rows
            standard = (piece[...] - mean) * scale
            out_ref[lanes, slot * PIECE : (slot + 1) * PIECE] = standard.T.astype(jnp.bfloat16)


def slab_standard(slab, order):
    return pl.pallas_call(
        slab_kernel,
        out_shape=jax.ShapeDtypeStruct((ROWS_DEV, TOKENS), jnp.bfloat16),
        in_specs=[pl.BlockSpec(memory_space=pltpu.SMEM), pl.BlockSpec(memory_space=pltpu.VMEM)],
        out_specs=pl.BlockSpec(memory_space=pltpu.VMEM),
        scratch_shapes=[
            pltpu.VMEM((ROWS_DEV // 128, TOKENS, 128), jnp.float32),
            pltpu.VMEM((PIECE, 128), jnp.float32),
        ],
        compiler_params=pltpu.CompilerParams(vmem_limit_bytes=24 * 2**20),
        cost_estimate=pl.CostEstimate(flops=8 * TOKENS * ROWS_DEV, bytes_accessed=4 * TOKENS * ROWS_DEV, transcendentals=0),
    )(order, slab)


def columns_kernel(slab_ref, own, x1, x2, y1, y2, x3, x4, y3, y4, out_ref, standard):
    def tiles(pieces, n_tiles, offset):
        @pl.loop(0, n_tiles)
        def _(j):
            def load(slot):
                ref, row, shift = pieces[slot]
                lanes = pl.ds(pl.multiple_of(j * TILE + shift, TILE), TILE)
                return ref[row : row + PIECE, lanes].astype(jnp.float32)

            total = jnp.zeros((8, TILE), jnp.float32)
            for slot in range(16):
                total += jnp.sum(load(slot).reshape(PIECE // 8, 8, TILE), axis=0)
            mean = jnp.sum(total, axis=0, keepdims=True) / TOKENS
            total = jnp.zeros((8, TILE), jnp.float32)
            for slot in range(16):
                centered = load(slot) - mean
                total += jnp.sum((centered * centered).reshape(PIECE // 8, 8, TILE), axis=0)
            spread = jnp.sqrt(jnp.sum(total, axis=0, keepdims=True) / TOKENS + EPS)
            scale = 1.0 / spread
            for slot in range(16):
                standard[slot * PIECE : (slot + 1) * PIECE, :] = ((load(slot) - mean) * scale).astype(jnp.bfloat16)
            product = jnp.dot(slab_ref[...], standard[...], preferred_element_type=jnp.float32)
            lanes = pl.ds(pl.multiple_of(j * TILE + offset, TILE), TILE)
            out_ref[:, lanes] = (product / TOKENS).astype(jnp.bfloat16)

    def at(ref, i, shift=0):
        return (ref, i * PIECE, shift)

    tiles(
        [at(own, 0), at(x1, 0), at(x2, 0), at(x2, 1)]
        + [at(y1, 0), at(x3, 0), at(x4, 0), at(x4, 3)]
        + [at(y2, 0), at(x3, 1), at(x4, 1), at(x4, 4)]
        + [at(y2, 1), at(x3, 2), at(x4, 2), at(x4, 5)],
        FIRST // TILE,
        0,
    )
    width = own.shape[1]
    tiles(
        [at(own, 0, FIRST), at(x1, 0, FIRST), at(x2, 0, FIRST), at(x2, 1, FIRST)]
        + [at(y3, i) for i in range(4)]
        + [at(y4, i) for i in range(8)],
        (width - FIRST) // TILE,
        FIRST,
    )


def correlate(slab, pieces):
    width = pieces[0].shape[1]
    return pl.pallas_call(
        columns_kernel,
        out_shape=jax.ShapeDtypeStruct((ROWS_DEV, width), jnp.bfloat16),
        in_specs=[pl.BlockSpec(memory_space=pltpu.VMEM)] * (1 + len(pieces)),
        out_specs=pl.BlockSpec(memory_space=pltpu.VMEM),
        scratch_shapes=[pltpu.VMEM((TOKENS, TILE), jnp.bfloat16)],
        compiler_params=pltpu.CompilerParams(vmem_limit_bytes=24 * 2**20),
        cost_estimate=pl.CostEstimate(
            flops=2 * TOKENS * ROWS_DEV * width, bytes_accessed=2 * TOKENS * (ROWS_DEV + width), transcendentals=0
        ),
    )(slab, *pieces)


def per_device(activations):
    slab_width = ROWS_DEV * 16
    slab_own = activations[:, :slab_width]
    slab_other = lax.ppermute(slab_own, "yl", [(0, 1), (1, 0)])
    first = lax.axis_index("yl") == 0
    slab_pair = jnp.concatenate(
        [jnp.where(first, slab_own, slab_other), jnp.where(first, slab_other, slab_own)], axis=0
    )

    own = lax.all_to_all(activations, ("yl", "z", "c"), split_axis=1, concat_axis=0, tiled=True)
    x1 = exchange(own, "x", 0)
    own_first = own[:, :FIRST]
    y1 = exchange(own_first, "yh", 0)
    slab_local = lax.all_to_all(slab_pair, ("x", "yh"), split_axis=1, concat_axis=0, tiled=True)
    slab_all = lax.all_gather(slab_local, ("z", "c"), axis=0, tiled=True)
    x2 = exchange(jnp.concatenate([own, x1], axis=0), "x", 1)
    y2 = exchange(jnp.concatenate([own_first, y1], axis=0), "yh", 1)
    rest = jnp.concatenate([own[:, FIRST:], x1[:, FIRST:], x2[:, FIRST:]], axis=0)
    three = jnp.concatenate([y1, y2], axis=0)
    x3 = exchange(three, "x", 0)
    y3 = exchange(rest, "yh", 0)
    x4 = exchange(jnp.concatenate([three, x3], axis=0), "x", 1)
    y4 = exchange(jnp.concatenate([rest, y3], axis=0), "yh", 1)

    near = jnp.where(lax.axis_index("c") == 0, 1, 3)
    flips = jnp.stack([0 * near, near, 4 - near, 2 + 0 * near])
    x_of = lax.axis_index("x") ^ flips
    y_of = lax.axis_index("yh") ^ flips
    order = (x_of[None, :] * 4 + y_of[:, None]).reshape(16).astype(jnp.int32)
    slab = slab_standard(slab_all, order)
    return correlate(slab, [own, x1, x2, y1, y2, x3, x4, y3, y4])


def solution(mesh):
    fine = Mesh(mesh.devices.reshape(4, 4, 2, 8, 2), ("x", "yh", "yl", "z", "c"))
    in_specs = (P(("x", "yh", "yl", "z", "c"), None),)
    out_specs = P(("x", "yh"), ("yl", "z", "c"))
    return jax.shard_map(per_device, mesh=fine, in_specs=in_specs, out_specs=out_specs, check_vma=False)
```

```python
import jax
import jax.numpy as jnp
import numpy as np
from jax import lax
from jax.experimental import pallas as pl
from jax.experimental.pallas import tpu as pltpu
from jax.sharding import Mesh, PartitionSpec as P

ROWS_DEV = 512
EPS = 1e-06
TOKENS = 2048
HALF = ROWS_DEV // 2
FIRST = 1280
PIECE = 128
TILE = 256
ALL = ("x", "yh", "yl", "z", "c")

SLOTS = [(0, 0), (1, 0), (2, 0), (3, 0), (0, 1), (1, 1), (0, 2), (1, 2), (0, 3), (1, 3)]
SLOTS += [(2, 1), (3, 1), (2, 2), (3, 2), (2, 3), (3, 3)]


def exchange(values, axis, step):
    perm = []
    for i in range(4):
        for core in range(2):
            flip = 1 if core == step else 3
            perm.append((i * 2 + core, (i ^ flip) * 2 + core))
    return lax.ppermute(values, (axis, "c"), perm)


def swap_places(values, flip):
    perm = [(a * 16 + b, b * 16 + (a ^ flip)) for a in range(16) for b in range(16)]
    return lax.ppermute(values, ("x", "yh", "yl", "z"), perm)


EVEN = [1, 0, 3, 2, 5, 4, 7, 6]
ODD = [7, 2, 1, 4, 3, 6, 5, 0]
Z_STEPS = [([3, 6, 5, 0, 7, 2, 1, 4], [5, 4, 7, 6, 1, 0, 3, 2]), (ODD, EVEN), (EVEN, ODD)]


def z_exchange(values, step):
    perm = [(z * 2 + core, Z_STEPS[step][core][z] * 2 + core) for z in range(8) for core in range(2)]
    return jnp.concatenate([values, lax.ppermute(values, ("z", "c"), perm)], axis=0)


def z_places():
    held = {(z, core): [z] for z in range(8) for core in range(2)}
    for step in range(3):
        held = {(z, core): held[z, core] + held[Z_STEPS[step][core][z], core] for z, core in held}
    return np.array([[np.argsort(held[z, core]) for core in range(2)] for z in range(8)], np.int32)


def fold(values):
    return jnp.sum(values.reshape(values.shape[0] // 8, 8, values.shape[1]), axis=0)


def slab_kernel(place_ref, mine_ref, other_ref, out_ref, sums_ref):
    n = TOKENS // PIECE
    for i, ref in enumerate((mine_ref, other_ref)):

        def rows(j, ref=ref):
            return ref[pl.ds(pl.multiple_of(j * PIECE, PIECE), PIECE), :].astype(jnp.float32)

        def add(j, total):
            return total + fold(rows(j))

        zero = jnp.zeros((8, HALF), jnp.float32)
        mean = jnp.sum(lax.fori_loop(0, n, add, zero), axis=0, keepdims=True) / TOKENS

        def square(j, total):
            centered = rows(j) - mean
            return total + fold(centered * centered)

        variance = jnp.sum(lax.fori_loop(0, n, square, zero), axis=0, keepdims=True) / TOKENS
        scale = 1.0 / jnp.sqrt(variance + EPS)
        units = pl.ds(pl.multiple_of(place_ref[2, i] * HALF, HALF), HALF)
        sums = jnp.zeros((HALF, 1), jnp.float32)
        for slot in range(n):
            standard = ((rows(place_ref[i, slot]) - mean) * scale).T.astype(jnp.bfloat16)
            out_ref[units, slot * PIECE : (slot + 1) * PIECE] = standard
            sums += jnp.sum(standard.astype(jnp.float32), axis=1, keepdims=True)
        sums_ref[units, :] = jnp.broadcast_to(sums, (HALF, 128))


def call(kernel, outs, in_specs, scratch, flops, moved, args):
    return pl.pallas_call(
        kernel,
        out_shape=outs,
        in_specs=in_specs,
        out_specs=[pl.BlockSpec(memory_space=pltpu.VMEM)] * len(outs),
        scratch_shapes=scratch,
        compiler_params=pltpu.CompilerParams(vmem_limit_bytes=32 * 2**20),
        cost_estimate=pl.CostEstimate(flops=flops, bytes_accessed=moved, transcendentals=0),
    )(*args)


VMEM = pl.BlockSpec(memory_space=pltpu.VMEM)


def slab_standard(mine, other, place):
    return call(
        slab_kernel,
        [jax.ShapeDtypeStruct((ROWS_DEV, TOKENS), jnp.bfloat16), jax.ShapeDtypeStruct((ROWS_DEV, 128), jnp.float32)],
        [pl.BlockSpec(memory_space=pltpu.SMEM), VMEM, VMEM],
        [],
        8 * TOKENS * ROWS_DEV,
        4 * TOKENS * ROWS_DEV,
        (place, mine, other),
    )


def tile_at(ref, part, j, shift):
    lanes = pl.ds(pl.multiple_of(j * TILE + shift, TILE), TILE)
    return ref[part * PIECE : (part + 1) * PIECE, lanes].astype(jnp.float32)


def early_kernel(slab_ref, own, x1, x2, y1, y2, x3, y3, acc_ref, pivot_ref, square_ref, shifted):
    width = own.shape[1]

    def tiles(pieces, n_tiles, offset, spans):
        @pl.loop(0, n_tiles)
        def _(j):
            lanes = pl.ds(pl.multiple_of(j * TILE + offset, TILE), TILE)
            total = jnp.zeros((8, TILE), jnp.float32)
            for ref, part, shift in pieces:
                total += fold(tile_at(ref, part, j, shift))
            pivot = jnp.sum(total, axis=0, keepdims=True) / (len(pieces) * PIECE)
            square = jnp.zeros((8, TILE), jnp.float32)
            for i, (ref, part, shift) in enumerate(pieces):
                values = tile_at(ref, part, j, shift) - pivot
                square += fold(values * values)
                shifted[i * PIECE : (i + 1) * PIECE, :] = values.astype(jnp.bfloat16)
            pivot_ref[:, lanes] = jnp.broadcast_to(pivot, (8, TILE))
            square_ref[:, lanes] = square
            acc = None
            row = 0
            for first, size in spans:
                part = jnp.dot(
                    slab_ref[:, first : first + size], shifted[row : row + size, :], preferred_element_type=jnp.float32
                )
                acc = part if acc is None else acc + part
                row += size
            acc_ref[:, lanes] = acc

    tiles(
        [(own, 0, 0), (x1, 0, 0), (x2, 0, 0), (x2, 1, 0), (y1, 0, 0)]
        + [(x3, 0, 0), (y2, 0, 0), (x3, 1, 0), (y2, 1, 0), (x3, 2, 0)],
        FIRST // TILE,
        0,
        [(0, 1280)],
    )
    tiles(
        [(own, 0, FIRST), (x1, 0, FIRST), (x2, 0, FIRST), (x2, 1, FIRST)] + [(y3, i, 0) for i in range(4)],
        (width - FIRST) // TILE,
        FIRST,
        [(0, 768), (1280, 256)],
    )


def late_kernel(slab_ref, sums_ref, acc_ref, pivot_ref, square_ref, x4, y4, out_ref, shifted):
    width = acc_ref.shape[1]

    def tiles(pieces, n_tiles, offset, spans):
        @pl.loop(0, n_tiles)
        def _(j):
            lanes = pl.ds(pl.multiple_of(j * TILE + offset, TILE), TILE)
            pivot = pivot_ref[0:1, lanes]
            total = jnp.zeros((8, TILE), jnp.float32)
            square = square_ref[:, lanes]
            for i, (ref, part) in enumerate(pieces):
                values = tile_at(ref, part, j, 0) - pivot
                total += fold(values)
                square += fold(values * values)
                shifted[i * PIECE : (i + 1) * PIECE, :] = values.astype(jnp.bfloat16)
            delta = jnp.sum(total, axis=0, keepdims=True) / TOKENS
            variance = jnp.sum(square, axis=0, keepdims=True) / TOKENS - delta * delta
            scale = 1.0 / (jnp.sqrt(jnp.maximum(variance, 0.0) + EPS) * TOKENS)
            acc = acc_ref[:, lanes]
            row = 0
            for first, size in spans:
                acc += jnp.dot(
                    slab_ref[:, first : first + size], shifted[row : row + size, :], preferred_element_type=jnp.float32
                )
                row += size
            out_ref[:, lanes] = ((acc - sums_ref[:, 0:1] * delta) * scale).astype(jnp.bfloat16)

    tiles([(x4, 0), (x4, 3), (x4, 1), (x4, 4), (x4, 2), (x4, 5)], FIRST // TILE, 0, [(1280, 768)])
    tiles(
        [(y4, 0), (y4, 1), (y4, 4), (y4, 5), (y4, 2), (y4, 3), (y4, 6), (y4, 7)],
        (width - FIRST) // TILE,
        FIRST,
        [(768, 512), (1536, 512)],
    )


def per_device(activations):
    together = lax.optimization_barrier
    tok, units = activations.shape
    n_col = 32
    width = units // n_col
    with_slab = jnp.concatenate(
        [activations.reshape(tok, n_col, width), activations[:, : n_col * HALF].reshape(tok, n_col, HALF)], axis=2
    )
    block = lax.all_to_all(
        with_slab.reshape(tok, n_col * (width + HALF)), ("yl", "z", "c"), split_axis=1, concat_axis=0, tiled=True
    )
    own, own_first, slab0 = block[:, :width], block[:, :FIRST], block[:, width:]
    y1 = exchange(own_first, "yh", 0)
    x1 = exchange(own, "x", 0)
    slab1 = jnp.concatenate([swap_places(slab0, 0), swap_places(slab0, 8)], axis=0)
    x1, y1, slab1 = together((x1, y1, slab1))
    y2 = exchange(jnp.concatenate([own_first, y1], axis=0), "yh", 1)
    x2 = exchange(jnp.concatenate([own, x1], axis=0), "x", 1)
    slab2 = z_exchange(z_exchange(slab1, 0), 1)
    x2, y2, slab2 = together((x2, y2, slab2))
    rest = jnp.concatenate([own[:, FIRST:], x1[:, FIRST:], x2[:, FIRST:]], axis=0)
    three = jnp.concatenate([y1, y2], axis=0)
    y3 = exchange(rest, "yh", 0)
    x3 = exchange(three, "x", 0)
    mine = z_exchange(slab2, 2)
    x3, y3, mine = together((x3, y3, mine))
    other = lax.ppermute(mine, "c", [(0, 1), (1, 0)])
    rest = jnp.concatenate([rest, y3], axis=0)
    y4 = exchange(rest, "yh", 1)
    three, x3, rest = together((three, x3, rest))
    x4 = exchange(jnp.concatenate([three, x3], axis=0), "x", 1)

    near = jnp.where(lax.axis_index("c") == 0, 1, 3)
    flips = [0, near, 4 - near, 2]
    token_of = jnp.stack(
        [(lax.axis_index("x") ^ flips[i]) * 4 + (lax.axis_index("yh") ^ flips[j]) for i, j in SLOTS]
    )
    z, core = lax.axis_index("z"), lax.axis_index("c")
    swapped = (token_of // 8) ^ lax.axis_index("yl")
    tables = jnp.asarray(z_places())[z]
    place = jnp.stack(
        [tables[core][token_of % 8] * 2 + swapped, tables[1 - core][token_of % 8] * 2 + swapped]
        + [jnp.where(jnp.arange(16) == 0, core, 1 - core)]
    )
    slab, sums = slab_standard(mine, other, place.astype(jnp.int32))

    wide = jax.ShapeDtypeStruct((8, width), jnp.float32)
    acc, pivot, square = call(
        early_kernel,
        [jax.ShapeDtypeStruct((ROWS_DEV, width), jnp.float32), wide, wide],
        [VMEM] * 8,
        [pltpu.VMEM((1280, TILE), jnp.bfloat16)],
        TOKENS * ROWS_DEV * width,
        4 * ROWS_DEV * width,
        (slab, own, x1, x2, y1, y2, x3, y3),
    )
    (out,) = call(
        late_kernel,
        [jax.ShapeDtypeStruct((ROWS_DEV, width), jnp.bfloat16)],
        [VMEM] * 7,
        [pltpu.VMEM((1024, TILE), jnp.bfloat16)],
        TOKENS * ROWS_DEV * width,
        4 * ROWS_DEV * width,
        (slab, sums, acc, pivot, square, x4, y4),
    )
    return out


def solution(mesh):
    fine = Mesh(mesh.devices.reshape(4, 4, 2, 8, 2), ALL)
    out_specs = P(("x", "yh"), ("yl", "z", "c"))
    return jax.shard_map(per_device, mesh=fine, in_specs=(P(ALL, None),), out_specs=out_specs, check_vma=False)
```

```python
import jax
import jax.numpy as jnp
import numpy as np
from jax import lax
from jax.experimental import pallas as pl
from jax.experimental.pallas import tpu as pltpu
from jax.sharding import Mesh, PartitionSpec as P

ROWS_DEV = 512
EPS = 1e-06
TOKENS = 2048
FIRST = 1408
PIECE = 128
TILE = 256
ALL = ("x", "yh", "yl", "z", "c")

SLOTS = [(0, 0), (1, 0), (2, 0), (3, 0), (0, 1), (1, 1), (0, 2), (1, 2), (0, 3), (1, 3)]
SLOTS += [(2, 1), (3, 1), (2, 2), (3, 2), (2, 3), (3, 3)]


def exchange(values, axis, step):
    perm = []
    for i in range(4):
        for core in range(2):
            flip = 1 if core == step else 3
            perm.append((i * 2 + core, (i ^ flip) * 2 + core))
    return lax.ppermute(values, (axis, "c"), perm)


def swap_places(values):
    perm = [(a * 32 + y * 16 + b, b * 32 + y * 16 + a) for a in range(16) for y in range(2) for b in range(16)]
    return lax.ppermute(values, ALL, perm)


EVEN = [1, 0, 3, 2, 5, 4, 7, 6]
ODD = [7, 2, 1, 4, 3, 6, 5, 0]
Z_STEPS = [([3, 6, 5, 0, 7, 2, 1, 4], [5, 4, 7, 6, 1, 0, 3, 2]), (ODD, EVEN), (EVEN, ODD)]


def z_permute(values, step):
    perm = [(z * 2 + core, Z_STEPS[step][core][z] * 2 + core) for z in range(8) for core in range(2)]
    return lax.ppermute(values, ("z", "c"), perm)


def z_places():
    held = {(z, core): [z] for z in range(8) for core in range(2)}
    for step in range(3):
        held = {(z, core): held[z, core] + held[Z_STEPS[step][core][z], core] for z, core in held}
    return np.array([[np.argsort(held[z, core]) for core in range(2)] for z in range(8)], np.int32)


def fold(values):
    return jnp.sum(values.reshape(values.shape[0] // 8, 8, values.shape[1]), axis=0)


def slab_kernel(place_ref, mine2_ref, mine3_ref, other2_ref, other3_ref, out_ref, sums_ref, whole):
    n = TOKENS // PIECE
    for first in range(0, ROWS_DEV, TILE):
        lanes = slice(first, first + TILE)
        total = jnp.zeros((8, TILE), jnp.float32)
        for part, ref in enumerate((mine2_ref, mine3_ref, other2_ref, other3_ref)):

            def add(i, total, part=part, ref=ref):
                start = pl.multiple_of(i * PIECE, PIECE)
                values = ref[pl.ds(start, PIECE), lanes]
                whole[pl.ds(start + part * (TOKENS // 4), PIECE), lanes] = values
                return total + fold(values.astype(jnp.float32))

            total = lax.fori_loop(0, n // 4, add, total)
        mean = jnp.sum(total, axis=0, keepdims=True) / TOKENS

        def rows(i):
            return whole[pl.ds(pl.multiple_of(i * PIECE, PIECE), PIECE), lanes].astype(jnp.float32)

        def square(i, total):
            centered = rows(i) - mean
            return total + fold(centered * centered)

        variance = jnp.sum(lax.fori_loop(0, n, square, jnp.zeros((8, TILE), jnp.float32)), axis=0, keepdims=True) / TOKENS
        scale = 1.0 / jnp.sqrt(variance + EPS)
        sums = jnp.zeros((TILE, 1), jnp.float32)
        for slot in range(n):
            standard = ((rows(place_ref[slot]) - mean) * scale).T.astype(jnp.bfloat16)
            out_ref[first : first + TILE, slot * PIECE : (slot + 1) * PIECE] = standard
            sums += jnp.sum(standard.astype(jnp.float32), axis=1, keepdims=True)
        sums_ref[first : first + TILE, :] = jnp.broadcast_to(sums, (TILE, 128))


def call(kernel, outs, in_specs, scratch, flops, moved, args):
    return pl.pallas_call(
        kernel,
        out_shape=outs,
        in_specs=in_specs,
        out_specs=[pl.BlockSpec(memory_space=pltpu.VMEM)] * len(outs),
        scratch_shapes=scratch,
        compiler_params=pltpu.CompilerParams(vmem_limit_bytes=32 * 2**20),
        cost_estimate=pl.CostEstimate(flops=flops // 64, bytes_accessed=moved // 64, transcendentals=0),
    )(*args)


VMEM = pl.BlockSpec(memory_space=pltpu.VMEM)


def slab_standard(quarters, place):
    return call(
        slab_kernel,
        [jax.ShapeDtypeStruct((ROWS_DEV, TOKENS), jnp.bfloat16), jax.ShapeDtypeStruct((ROWS_DEV, 128), jnp.float32)],
        [pl.BlockSpec(memory_space=pltpu.SMEM)] + [VMEM] * 4,
        [pltpu.VMEM((TOKENS, ROWS_DEV), jnp.bfloat16)],
        8 * TOKENS * ROWS_DEV,
        4 * TOKENS * ROWS_DEV,
        (place, *quarters),
    )


def tile_at(ref, part, lanes):
    return ref[pl.ds(pl.multiple_of(part * PIECE, PIECE), PIECE), lanes].astype(jnp.float32)


def over_tiles(width, body):
    whole = width // TILE

    @pl.loop(0, whole)
    def _(j):
        body(j * TILE, TILE)

    if width % TILE:
        body(whole * TILE, width % TILE)


def at(start, size):
    return pl.ds(pl.multiple_of(start, 128), size)


def product(slab_ref, shifted, spans, size):
    acc, row = None, 0
    for first, depth in spans:
        part = jnp.dot(
            slab_ref[:, first : first + depth], shifted[row : row + depth, :size], preferred_element_type=jnp.float32
        )
        acc = part if acc is None else acc + part
        row += depth
    return acc


def early_kernel(slab_ref, own, x1, x2, y1, y2, x3, y3, acc_ref, pivot_ref, square_ref, shifted):
    width = own.shape[1]

    def tiles(pieces, offset, columns, spans):
        def body(start, size):
            lanes = at(start + offset, size)

            def load(piece):
                ref, part, whole = piece
                return tile_at(ref, part, lanes if whole else at(start, size))

            total = jnp.zeros((8, size), jnp.float32)
            for piece in pieces:
                total += fold(load(piece))
            pivot = jnp.sum(total, axis=0, keepdims=True) / (len(pieces) * PIECE)
            square = jnp.zeros((8, size), jnp.float32)
            for i, piece in enumerate(pieces):
                values = load(piece) - pivot
                square += fold(values * values)
                shifted[i * PIECE : (i + 1) * PIECE, :size] = values.astype(jnp.bfloat16)
            pivot_ref[:, lanes] = jnp.broadcast_to(pivot, (8, size))
            square_ref[:, lanes] = square
            acc_ref[:, lanes] = product(slab_ref, shifted, spans, size)

        over_tiles(columns, body)

    near = [(own, 0, True), (x1, 0, True), (x2, 0, True), (x2, 1, True)]
    tiles(
        near
        + [(y1, 0, False), (x3, 0, False), (y2, 0, False), (x3, 1, False), (y2, 1, False), (x3, 2, False)],
        0,
        FIRST,
        [(0, 1280)],
    )
    tiles(near + [(y3, i, False) for i in range(4)], FIRST, width - FIRST, [(0, 768), (1280, 256)])


def late_kernel(slab_ref, sums_ref, acc_ref, pivot_ref, square_ref, x4, y4, out_ref, shifted):
    width = acc_ref.shape[1]

    def tiles(pieces, offset, columns, spans):
        def body(start, size):
            lanes = at(start + offset, size)
            pivot = pivot_ref[0:1, lanes]
            total = jnp.zeros((8, size), jnp.float32)
            square = square_ref[:, lanes]
            for i, (ref, part) in enumerate(pieces):
                values = tile_at(ref, part, at(start, size)) - pivot
                total += fold(values)
                square += fold(values * values)
                shifted[i * PIECE : (i + 1) * PIECE, :size] = values.astype(jnp.bfloat16)
            delta = jnp.sum(total, axis=0, keepdims=True) / TOKENS
            variance = jnp.sum(square, axis=0, keepdims=True) / TOKENS - delta * delta
            scale = 1.0 / (jnp.sqrt(jnp.maximum(variance, 0.0) + EPS) * TOKENS)
            acc = acc_ref[:, lanes] + product(slab_ref, shifted, spans, size)
            out_ref[:, lanes] = ((acc - sums_ref[:, 0:1] * delta) * scale).astype(jnp.bfloat16)

        over_tiles(columns, body)

    tiles([(x4, i) for i in (0, 3, 1, 4, 2, 5)], 0, FIRST, [(1280, 768)])
    tiles([(y4, i) for i in (0, 1, 4, 5, 2, 3, 6, 7)], FIRST, width - FIRST, [(768, 512), (1536, 512)])


def per_device(activations):
    together = lax.optimization_barrier
    tok, units = activations.shape
    n_col = 32
    width = units // n_col
    slab = activations[:, : 16 * ROWS_DEV].reshape(tok, 1, 16, ROWS_DEV)
    with_slab = jnp.concatenate(
        [activations.reshape(tok, 2, 16, width), jnp.broadcast_to(slab, (tok, 2, 16, ROWS_DEV))], axis=3
    )
    block = lax.all_to_all(
        with_slab.reshape(tok, n_col * (width + ROWS_DEV)), ("yl", "z", "c"), split_axis=1, concat_axis=0, tiled=True
    )
    own, own_first, slab0 = block[:, :width], block[:, :FIRST], block[:, width:]
    y1 = exchange(own_first, "yh", 0)
    x1 = exchange(own, "x", 0)
    slab0 = swap_places(slab0)
    x1, y1, slab0 = together((x1, y1, slab0))
    y2 = exchange(jnp.concatenate([own_first, y1], axis=0), "yh", 1)
    x2 = exchange(jnp.concatenate([own, x1], axis=0), "x", 1)
    slab1 = jnp.concatenate([slab0, z_permute(slab0, 0)], axis=0)
    slab2 = z_permute(slab1, 1)
    x2, y2, slab1, slab2 = together((x2, y2, slab1, slab2))
    rest = jnp.concatenate([own[:, FIRST:], x1[:, FIRST:], x2[:, FIRST:]], axis=0)
    three = jnp.concatenate([y1, y2], axis=0)
    y3 = exchange(rest, "yh", 0)
    x3 = exchange(three, "x", 0)
    slab2 = jnp.concatenate([slab1, slab2], axis=0)
    slab3 = z_permute(slab2, 2)
    x3, y3, slab2, slab3 = together((x3, y3, slab2, slab3))
    rest = jnp.concatenate([rest, y3], axis=0)
    y4 = exchange(rest, "yh", 1)
    three, x3, rest = together((three, x3, rest))
    x4 = exchange(jnp.concatenate([three, x3], axis=0), "x", 1)

    quarters = [slab2, slab3] + [lax.ppermute(part, "c", [(0, 1), (1, 0)]) for part in (slab2, slab3)]

    near = jnp.where(lax.axis_index("c") == 0, 1, 3)
    flips = [0, near, 4 - near, 2]
    token_of = jnp.stack(
        [(lax.axis_index("x") ^ flips[i]) * 4 + (lax.axis_index("yh") ^ flips[j]) for i, j in SLOTS]
    )
    core = lax.axis_index("c")
    table = jnp.asarray(z_places())[lax.axis_index("z")]
    table = jnp.where(core == 0, table, table[::-1])
    place = jnp.where(token_of % 2 == core, table[0][token_of // 2], table[1][token_of // 2] + 8)
    slab, sums = slab_standard(quarters, place.astype(jnp.int32))

    wide = jax.ShapeDtypeStruct((8, width), jnp.float32)
    acc, pivot, square = call(
        early_kernel,
        [jax.ShapeDtypeStruct((ROWS_DEV, width), jnp.float32), wide, wide],
        [VMEM] * 8,
        [pltpu.VMEM((1280, TILE), jnp.bfloat16)],
        TOKENS * ROWS_DEV * width,
        4 * ROWS_DEV * width,
        (slab, own, x1, x2, y1, y2, x3, y3),
    )
    (out,) = call(
        late_kernel,
        [jax.ShapeDtypeStruct((ROWS_DEV, width), jnp.bfloat16)],
        [VMEM] * 7,
        [pltpu.VMEM((1024, TILE), jnp.bfloat16)],
        TOKENS * ROWS_DEV * width,
        4 * ROWS_DEV * width,
        (slab, sums, acc, pivot, square, x4, y4),
    )
    return out


def solution(mesh):
    fine = Mesh(mesh.devices.reshape(4, 4, 2, 8, 2), ALL)
    out_specs = P(("x", "yh"), ("yl", "z", "c"))
    return jax.shard_map(per_device, mesh=fine, in_specs=(P(ALL, None),), out_specs=out_specs, check_vma=False)
```

```python
import jax
import jax.numpy as jnp
import numpy as np
from jax import lax
from jax.experimental import pallas as pl
from jax.experimental.pallas import tpu as pltpu
from jax.sharding import Mesh, PartitionSpec as P

ROWS_DEV = 512
EPS = 1e-06
TOKENS = 2048
FIRST = 1408
PIECE = 128
TILE = 256
ALL = ("x", "yh", "yl", "z", "c")

SLOTS = [(0, 0), (1, 0), (2, 0), (3, 0), (0, 1), (1, 1), (0, 2), (1, 2), (0, 3), (1, 3)]
SLOTS += [(2, 1), (3, 1), (2, 2), (3, 2), (2, 3), (3, 3)]


def exchange(values, axis, step):
    perm = []
    for i in range(4):
        for core in range(2):
            flip = 1 if core == step else 3
            perm.append((i * 2 + core, (i ^ flip) * 2 + core))
    return lax.ppermute(values, (axis, "c"), perm)


def swap_places(values):
    perm = [(a * 32 + y * 16 + b, b * 32 + y * 16 + a) for a in range(16) for y in range(2) for b in range(16)]
    return lax.ppermute(values, ALL, perm)


EVEN = [1, 0, 3, 2, 5, 4, 7, 6]
ODD = [7, 2, 1, 4, 3, 6, 5, 0]
Z_STEPS = [([3, 6, 5, 0, 7, 2, 1, 4], [5, 4, 7, 6, 1, 0, 3, 2]), (ODD, EVEN), (EVEN, ODD)]


def z_permute(values, step):
    perm = [(z * 2 + core, Z_STEPS[step][core][z] * 2 + core) for z in range(8) for core in range(2)]
    return lax.ppermute(values, ("z", "c"), perm)


def z_places():
    held = {(z, core): [z] for z in range(8) for core in range(2)}
    for step in range(3):
        held = {(z, core): held[z, core] + held[Z_STEPS[step][core][z], core] for z, core in held}
    return np.array([[np.argsort(held[z, core]) for core in range(2)] for z in range(8)], np.int32)


def fold(values):
    return jnp.sum(values.reshape(values.shape[0] // 8, 8, values.shape[1]), axis=0)


def slab_kernel(place_ref, mine2_ref, mine3_ref, other2_ref, other3_ref, out_ref, sums_ref, whole):
    n = TOKENS // PIECE
    for first in range(0, ROWS_DEV, TILE):
        lanes = slice(first, first + TILE)
        total = jnp.zeros((8, TILE), jnp.float32)
        for part, ref in enumerate((mine2_ref, mine3_ref, other2_ref, other3_ref)):

            def add(i, total, part=part, ref=ref):
                start = pl.multiple_of(i * PIECE, PIECE)
                values = ref[pl.ds(start, PIECE), lanes]
                whole[pl.ds(start + part * (TOKENS // 4), PIECE), lanes] = values
                return total + fold(values.astype(jnp.float32))

            total = lax.fori_loop(0, n // 4, add, total)
        mean = jnp.sum(total, axis=0, keepdims=True) / TOKENS

        def rows(i):
            return whole[pl.ds(pl.multiple_of(i * PIECE, PIECE), PIECE), lanes].astype(jnp.float32)

        def square(i, total):
            centered = rows(i) - mean
            return total + fold(centered * centered)

        variance = jnp.sum(lax.fori_loop(0, n, square, jnp.zeros((8, TILE), jnp.float32)), axis=0, keepdims=True) / TOKENS
        scale = 1.0 / jnp.sqrt(variance + EPS)
        sums = jnp.zeros((TILE, 1), jnp.float32)
        for slot in range(n):
            standard = ((rows(place_ref[slot]) - mean) * scale).T.astype(jnp.bfloat16)
            out_ref[first : first + TILE, slot * PIECE : (slot + 1) * PIECE] = standard
            sums += jnp.sum(standard.astype(jnp.float32), axis=1, keepdims=True)
        sums_ref[first : first + TILE, :] = jnp.broadcast_to(sums, (TILE, 128))


def call(kernel, outs, in_specs, scratch, flops, moved, args):
    return pl.pallas_call(
        kernel,
        out_shape=outs,
        in_specs=in_specs,
        out_specs=[pl.BlockSpec(memory_space=pltpu.VMEM)] * len(outs),
        scratch_shapes=scratch,
        compiler_params=pltpu.CompilerParams(vmem_limit_bytes=32 * 2**20),
        cost_estimate=pl.CostEstimate(flops=flops // 64, bytes_accessed=moved // 64, transcendentals=0),
    )(*args)


VMEM = pl.BlockSpec(memory_space=pltpu.VMEM)


def slab_standard(quarters, place):
    return call(
        slab_kernel,
        [jax.ShapeDtypeStruct((ROWS_DEV, TOKENS), jnp.bfloat16), jax.ShapeDtypeStruct((ROWS_DEV, 128), jnp.float32)],
        [pl.BlockSpec(memory_space=pltpu.SMEM)] + [VMEM] * 4,
        [pltpu.VMEM((TOKENS, ROWS_DEV), jnp.bfloat16)],
        8 * TOKENS * ROWS_DEV,
        4 * TOKENS * ROWS_DEV,
        (place, *quarters),
    )


def tile_at(ref, part, lanes):
    return ref[pl.ds(pl.multiple_of(part * PIECE, PIECE), PIECE), lanes].astype(jnp.float32)


def over_tiles(width, scratch, body):
    pairs = width // (2 * TILE)

    @pl.loop(0, pairs)
    def _(j):
        for i in range(2):
            body((2 * j + i) * TILE, TILE, scratch[i])

    for i, start in enumerate(range(pairs * 2 * TILE, width, TILE)):
        body(start, min(TILE, width - start), scratch[i])


def at(start, size):
    return pl.ds(pl.multiple_of(start, 128), size)


def product(slab_ref, shifted, spans, size):
    acc, row = None, 0
    for first, depth in spans:
        part = jnp.dot(
            slab_ref[:, first : first + depth], shifted[row : row + depth, :size], preferred_element_type=jnp.float32
        )
        acc = part if acc is None else acc + part
        row += depth
    return acc


def early_kernel(slab_ref, own, x1, x2, y1, y2, x3, y3, acc_ref, pivot_ref, square_ref, *scratch):
    width = own.shape[1]

    def tiles(pieces, offset, columns, spans):
        def body(start, size, shifted):
            lanes = at(start + offset, size)

            def load(piece):
                ref, part, whole = piece
                return tile_at(ref, part, lanes if whole else at(start, size))

            total = jnp.zeros((8, size), jnp.float32)
            for piece in pieces:
                total += fold(load(piece))
            pivot = jnp.sum(total, axis=0, keepdims=True) / (len(pieces) * PIECE)
            square = jnp.zeros((8, size), jnp.float32)
            for i, piece in enumerate(pieces):
                values = load(piece) - pivot
                square += fold(values * values)
                shifted[i * PIECE : (i + 1) * PIECE, :size] = values.astype(jnp.bfloat16)
            pivot_ref[:, lanes] = jnp.broadcast_to(pivot, (8, size))
            square_ref[:, lanes] = square
            acc_ref[:, lanes] = product(slab_ref, shifted, spans, size)

        over_tiles(columns, scratch, body)

    near = [(own, 0, True), (x1, 0, True), (x2, 0, True), (x2, 1, True)]
    tiles(
        near
        + [(y1, 0, False), (x3, 0, False), (y2, 0, False), (x3, 1, False), (y2, 1, False), (x3, 2, False)],
        0,
        FIRST,
        [(0, 1280)],
    )
    tiles(near + [(y3, i, False) for i in range(4)], FIRST, width - FIRST, [(0, 768), (1280, 256)])


def late_kernel(slab_ref, sums_ref, acc_ref, pivot_ref, square_ref, x4, y4, out_ref, *scratch):
    width = acc_ref.shape[1]

    def tiles(pieces, offset, columns, spans):
        def body(start, size, shifted):
            lanes = at(start + offset, size)
            pivot = pivot_ref[0:1, lanes]
            total = jnp.zeros((8, size), jnp.float32)
            square = square_ref[:, lanes]
            for i, (ref, part) in enumerate(pieces):
                values = tile_at(ref, part, at(start, size)) - pivot
                total += fold(values)
                square += fold(values * values)
                shifted[i * PIECE : (i + 1) * PIECE, :size] = values.astype(jnp.bfloat16)
            delta = jnp.sum(total, axis=0, keepdims=True) / TOKENS
            variance = jnp.sum(square, axis=0, keepdims=True) / TOKENS - delta * delta
            scale = 1.0 / (jnp.sqrt(jnp.maximum(variance, 0.0) + EPS) * TOKENS)
            acc = acc_ref[:, lanes] + product(slab_ref, shifted, spans, size)
            out_ref[:, lanes] = ((acc - sums_ref[:, 0:1] * delta) * scale).astype(jnp.bfloat16)

        over_tiles(columns, scratch, body)

    tiles([(x4, i) for i in (0, 3, 1, 4, 2, 5)], 0, FIRST, [(1280, 768)])
    tiles([(y4, i) for i in (0, 1, 4, 5, 2, 3, 6, 7)], FIRST, width - FIRST, [(768, 512), (1536, 512)])


def per_device(activations):
    together = lax.optimization_barrier
    tok, units = activations.shape
    n_col = 32
    width = units // n_col
    slab = activations[:, : 16 * ROWS_DEV].reshape(tok, 1, 16, ROWS_DEV)
    with_slab = jnp.concatenate(
        [activations.reshape(tok, 2, 16, width), jnp.broadcast_to(slab, (tok, 2, 16, ROWS_DEV))], axis=3
    )
    block = lax.all_to_all(
        with_slab.reshape(tok, n_col * (width + ROWS_DEV)), ("yl", "z", "c"), split_axis=1, concat_axis=0, tiled=True
    )
    own, own_first, slab0 = block[:, :width], block[:, :FIRST], block[:, width:]
    y1 = exchange(own_first, "yh", 0)
    x1 = exchange(own, "x", 0)
    slab0 = swap_places(slab0)
    x1, y1, slab0 = together((x1, y1, slab0))
    y2 = exchange(jnp.concatenate([own_first, y1], axis=0), "yh", 1)
    x2 = exchange(jnp.concatenate([own, x1], axis=0), "x", 1)
    slab1 = jnp.concatenate([slab0, z_permute(slab0, 0)], axis=0)
    slab2 = z_permute(slab1, 1)
    rest = jnp.concatenate([own[:, FIRST:], x1[:, FIRST:], x2[:, FIRST:]], axis=0)
    x2, y2, rest, slab1, slab2 = together((x2, y2, rest, slab1, slab2))
    three = jnp.concatenate([y1, y2], axis=0)
    y3 = exchange(rest, "yh", 0)
    x3 = exchange(three, "x", 0)
    slab2 = jnp.concatenate([slab1, slab2], axis=0)
    slab3 = z_permute(slab2, 2)
    x3, y3, slab2, slab3 = together((x3, y3, slab2, slab3))
    rest = jnp.concatenate([rest, y3], axis=0)
    y4 = exchange(rest, "yh", 1)
    x4 = exchange(jnp.concatenate([three, x3], axis=0), "x", 1)

    quarters = [slab2, slab3] + [lax.ppermute(part, "c", [(0, 1), (1, 0)]) for part in (slab2, slab3)]

    near = jnp.where(lax.axis_index("c") == 0, 1, 3)
    flips = [0, near, 4 - near, 2]
    token_of = jnp.stack(
        [(lax.axis_index("x") ^ flips[i]) * 4 + (lax.axis_index("yh") ^ flips[j]) for i, j in SLOTS]
    )
    core = lax.axis_index("c")
    table = jnp.asarray(z_places())[lax.axis_index("z")]
    table = jnp.where(core == 0, table, table[::-1])
    place = jnp.where(token_of % 2 == core, table[0][token_of // 2], table[1][token_of // 2] + 8)
    slab, sums = slab_standard(quarters, place.astype(jnp.int32))

    wide = jax.ShapeDtypeStruct((8, width), jnp.float32)
    acc, pivot, square = call(
        early_kernel,
        [jax.ShapeDtypeStruct((ROWS_DEV, width), jnp.float32), wide, wide],
        [VMEM] * 8,
        [pltpu.VMEM((1280, TILE), jnp.bfloat16)] * 2,
        TOKENS * ROWS_DEV * width,
        4 * ROWS_DEV * width,
        (slab, own, x1, x2, y1, y2, x3, y3),
    )
    (out,) = call(
        late_kernel,
        [jax.ShapeDtypeStruct((ROWS_DEV, width), jnp.bfloat16)],
        [VMEM] * 7,
        [pltpu.VMEM((1024, TILE), jnp.bfloat16)] * 2,
        TOKENS * ROWS_DEV * width,
        4 * ROWS_DEV * width,
        (slab, sums, acc, pivot, square, x4, y4),
    )
    return out


def solution(mesh):
    fine = Mesh(mesh.devices.reshape(4, 4, 2, 8, 2), ALL)
    out_specs = P(("x", "yh"), ("yl", "z", "c"))
    return jax.shard_map(per_device, mesh=fine, in_specs=(P(ALL, None),), out_specs=out_specs, check_vma=False)
```

```python
import jax
import jax.numpy as jnp
import numpy as np
from jax import lax
from jax.experimental import pallas as pl
from jax.experimental.pallas import tpu as pltpu
from jax.sharding import Mesh, PartitionSpec as P

ROWS_DEV = 512
EPS = 1e-06
TOKENS = 2048
FIRST = 1408
PIECE = 128
TILE = 256
ALL = ("x", "yh", "yl", "z", "c")

SLOTS = [(0, 0), (1, 0), (2, 0), (3, 0), (0, 1), (1, 1), (2, 1), (0, 2), (1, 2), (2, 2)]
SLOTS += [(0, 3), (1, 3), (2, 3), (3, 3), (3, 1), (3, 2)]
N_EARLY = 13


def exchange(values, axis, step):
    perm = []
    for i in range(4):
        for core in range(2):
            flip = 1 if core == step else 3
            perm.append((i * 2 + core, (i ^ flip) * 2 + core))
    return lax.ppermute(values, (axis, "c"), perm)


def swap_places(values):
    perm = [(a * 32 + y * 16 + b, b * 32 + y * 16 + a) for a in range(16) for y in range(2) for b in range(16)]
    return lax.ppermute(values, ALL, perm)


EVEN = [1, 0, 3, 2, 5, 4, 7, 6]
ODD = [7, 2, 1, 4, 3, 6, 5, 0]
Z_STEPS = [([3, 6, 5, 0, 7, 2, 1, 4], [5, 4, 7, 6, 1, 0, 3, 2]), (ODD, EVEN), (EVEN, ODD)]


def z_permute(values, step):
    perm = [(z * 2 + core, Z_STEPS[step][core][z] * 2 + core) for z in range(8) for core in range(2)]
    return lax.ppermute(values, ("z", "c"), perm)


def z_places():
    held = {(z, core): [z] for z in range(8) for core in range(2)}
    for step in range(3):
        held = {(z, core): held[z, core] + held[Z_STEPS[step][core][z], core] for z, core in held}
    return np.array([[np.argsort(held[z, core]) for core in range(2)] for z in range(8)], np.int32)


def fold(values):
    return jnp.sum(values.reshape(values.shape[0] // 8, 8, values.shape[1]), axis=0)


def slab_kernel(place_ref, mine2_ref, mine3_ref, other2_ref, other3_ref, out_ref, sums_ref, whole):
    n = TOKENS // PIECE
    for first in range(0, ROWS_DEV, TILE):
        lanes = slice(first, first + TILE)
        total = jnp.zeros((8, TILE), jnp.float32)
        for part, ref in enumerate((mine2_ref, mine3_ref, other2_ref, other3_ref)):

            def add(i, total, part=part, ref=ref):
                start = pl.multiple_of(i * PIECE, PIECE)
                values = ref[pl.ds(start, PIECE), lanes]
                whole[pl.ds(start + part * (TOKENS // 4), PIECE), lanes] = values
                return total + fold(values.astype(jnp.float32))

            total = lax.fori_loop(0, n // 4, add, total)
        mean = jnp.sum(total, axis=0, keepdims=True) / TOKENS

        def rows(i):
            return whole[pl.ds(pl.multiple_of(i * PIECE, PIECE), PIECE), lanes].astype(jnp.float32)

        def square(i, total):
            centered = rows(i) - mean
            return total + fold(centered * centered)

        variance = jnp.sum(lax.fori_loop(0, n, square, jnp.zeros((8, TILE), jnp.float32)), axis=0, keepdims=True) / TOKENS
        scale = 1.0 / jnp.sqrt(variance + EPS)
        sums = jnp.zeros((TILE, 1), jnp.float32)
        for slot in range(n):
            standard = ((rows(place_ref[slot]) - mean) * scale).T.astype(jnp.bfloat16)
            out_ref[first : first + TILE, slot * PIECE : (slot + 1) * PIECE] = standard
            sums += jnp.sum(standard.astype(jnp.float32), axis=1, keepdims=True)
        sums_ref[first : first + TILE, :] = jnp.broadcast_to(sums, (TILE, 128))


def call(kernel, outs, in_specs, scratch, flops, moved, args):
    return pl.pallas_call(
        kernel,
        out_shape=outs,
        in_specs=in_specs,
        out_specs=[pl.BlockSpec(memory_space=pltpu.VMEM)] * len(outs),
        scratch_shapes=scratch,
        compiler_params=pltpu.CompilerParams(vmem_limit_bytes=32 * 2**20),
        cost_estimate=pl.CostEstimate(flops=flops // 64, bytes_accessed=moved // 64, transcendentals=0),
    )(*args)


VMEM = pl.BlockSpec(memory_space=pltpu.VMEM)


def slab_standard(quarters, place):
    return call(
        slab_kernel,
        [jax.ShapeDtypeStruct((ROWS_DEV, TOKENS), jnp.bfloat16), jax.ShapeDtypeStruct((ROWS_DEV, 128), jnp.float32)],
        [pl.BlockSpec(memory_space=pltpu.SMEM)] + [VMEM] * 4,
        [pltpu.VMEM((TOKENS, ROWS_DEV), jnp.bfloat16)],
        8 * TOKENS * ROWS_DEV,
        4 * TOKENS * ROWS_DEV,
        (place, *quarters),
    )


def tile_at(ref, part, lanes):
    return ref[pl.ds(pl.multiple_of(part * PIECE, PIECE), PIECE), lanes].astype(jnp.float32)


def over_tiles(width, scratch, body):
    pairs = width // (2 * TILE)

    @pl.loop(0, pairs)
    def _(j):
        for i in range(2):
            body((2 * j + i) * TILE, TILE, scratch[i])

    for i, start in enumerate(range(pairs * 2 * TILE, width, TILE)):
        body(start, min(TILE, width - start), scratch[i])


def at(start, size):
    return pl.ds(pl.multiple_of(start, 128), size)


def product(slab_ref, shifted, spans, size):
    acc, row = None, 0
    for first, depth in spans:
        part = jnp.dot(
            slab_ref[:, first : first + depth], shifted[row : row + depth, :size], preferred_element_type=jnp.float32
        )
        acc = part if acc is None else acc + part
        row += depth
    return acc


def early_kernel(slab_ref, x0, x1, x2, x3, y0, y1, y2, r0, r1, r2, acc_ref, pivot_ref, square_ref, *scratch):
    width = x0.shape[1]

    def tiles(pieces, offset, columns, spans):
        def body(start, size, shifted):
            lanes = at(start + offset, size)

            def load(piece):
                ref, part = piece
                return tile_at(ref, part, at(start, size))

            total = jnp.zeros((8, size), jnp.float32)
            for piece in pieces:
                total += fold(load(piece))
            pivot = jnp.sum(total, axis=0, keepdims=True) / (len(pieces) * PIECE)
            square = jnp.zeros((8, size), jnp.float32)
            for i, piece in enumerate(pieces):
                values = load(piece) - pivot
                square += fold(values * values)
                shifted[i * PIECE : (i + 1) * PIECE, :size] = values.astype(jnp.bfloat16)
            pivot_ref[:, lanes] = jnp.broadcast_to(pivot, (8, size))
            square_ref[:, lanes] = square
            acc_ref[:, lanes] = product(slab_ref, shifted, spans, size)

        over_tiles(columns, scratch, body)

    first = [(x0, 0), (x1, 0), (x2, 0), (x3, 0)] + [((y0, y1, y2)[i], j - 1) for i, j in SLOTS[4:N_EARLY]]
    tiles(first, 0, FIRST, [(0, N_EARLY * PIECE)])
    others = [((r0, r1, r2)[j], i) for i, j in SLOTS[:10] + SLOTS[14:]]
    tiles(others, FIRST, width - FIRST, [(0, 10 * PIECE), (14 * PIECE, 2 * PIECE)])


def late_kernel(slab_ref, sums_ref, acc_ref, pivot_ref, square_ref, x4, y4, out_ref, *scratch):
    width = acc_ref.shape[1]

    def tiles(pieces, offset, columns, spans):
        def body(start, size, shifted):
            lanes = at(start + offset, size)
            pivot = pivot_ref[0:1, lanes]
            total = jnp.zeros((8, size), jnp.float32)
            square = square_ref[:, lanes]
            for i, (ref, part) in enumerate(pieces):
                values = tile_at(ref, part, at(start, size)) - pivot
                total += fold(values)
                square += fold(values * values)
                shifted[i * PIECE : (i + 1) * PIECE, :size] = values.astype(jnp.bfloat16)
            delta = jnp.sum(total, axis=0, keepdims=True) / TOKENS
            variance = jnp.sum(square, axis=0, keepdims=True) / TOKENS - delta * delta
            scale = 1.0 / (jnp.sqrt(jnp.maximum(variance, 0.0) + EPS) * TOKENS)
            acc = acc_ref[:, lanes] + product(slab_ref, shifted, spans, size)
            out_ref[:, lanes] = ((acc - sums_ref[:, 0:1] * delta) * scale).astype(jnp.bfloat16)

        over_tiles(columns, scratch, body)

    tiles([(x4, j - 1) for _, j in SLOTS[N_EARLY:]], 0, FIRST, [(N_EARLY * PIECE, 3 * PIECE)])
    tiles([(y4, i) for i, _ in SLOTS[10:14]], FIRST, width - FIRST, [(10 * PIECE, 4 * PIECE)])


def per_device(activations):
    together = lax.optimization_barrier
    tok, units = activations.shape
    n_col = 32
    width = units // n_col
    slab = activations[:, : 16 * ROWS_DEV].reshape(tok, 1, 16, ROWS_DEV)
    with_slab = jnp.concatenate(
        [activations.reshape(tok, 2, 16, width), jnp.broadcast_to(slab, (tok, 2, 16, ROWS_DEV))], axis=3
    )
    block = lax.all_to_all(
        with_slab.reshape(tok, n_col * (width + ROWS_DEV)), ("yl", "z", "c"), split_axis=1, concat_axis=0, tiled=True
    )
    own, own_first, slab0 = block[:, :width], block[:, :FIRST], block[:, width:]
    x1, x2 = exchange(own, "x", 0), exchange(own, "x", 1)
    y1, y2 = exchange(own_first, "yh", 0), exchange(own_first, "yh", 1)
    slab0 = swap_places(slab0)
    x1, x2, y1, y2, slab0 = together((x1, x2, y1, y2, slab0))
    x3 = exchange(x1, "x", 1)
    y3 = exchange(y1, "yh", 1)
    slab1 = jnp.concatenate([slab0, z_permute(slab0, 0)], axis=0)
    x3, y3, slab1 = together((x3, y3, slab1))
    three = jnp.concatenate([y1, y2, y3], axis=0)
    rest = jnp.concatenate([x[:, FIRST:] for x in (own, x1, x2, x3)], axis=0)
    three1, three2 = exchange(three, "x", 0), exchange(three, "x", 1)
    rest1, rest2 = exchange(rest, "yh", 0), exchange(rest, "yh", 1)
    slab2 = jnp.concatenate([slab1, z_permute(slab1, 1)], axis=0)
    slab3 = z_permute(slab2, 2)
    three1, three2, rest1, rest2, slab2, slab3 = together((three1, three2, rest1, rest2, slab2, slab3))
    three3 = exchange(three1, "x", 1)
    rest3 = exchange(rest1, "yh", 1)

    quarters = [slab2, slab3] + [lax.ppermute(part, "c", [(0, 1), (1, 0)]) for part in (slab2, slab3)]

    near = jnp.where(lax.axis_index("c") == 0, 1, 3)
    flips = [0, near, 4 - near, 2]
    token_of = jnp.stack(
        [(lax.axis_index("x") ^ flips[i]) * 4 + (lax.axis_index("yh") ^ flips[j]) for i, j in SLOTS]
    )
    core = lax.axis_index("c")
    table = jnp.asarray(z_places())[lax.axis_index("z")]
    table = jnp.where(core == 0, table, table[::-1])
    place = jnp.where(token_of % 2 == core, table[0][token_of // 2], table[1][token_of // 2] + 8)
    slab, sums = slab_standard(quarters, place.astype(jnp.int32))

    wide = jax.ShapeDtypeStruct((8, width), jnp.float32)
    acc, pivot, square = call(
        early_kernel,
        [jax.ShapeDtypeStruct((ROWS_DEV, width), jnp.float32), wide, wide],
        [VMEM] * 11,
        [pltpu.VMEM((N_EARLY * PIECE, TILE), jnp.bfloat16)] * 2,
        TOKENS * ROWS_DEV * width,
        4 * ROWS_DEV * width,
        (slab, own, x1, x2, x3, three, three1, three2, rest, rest1, rest2),
    )
    (out,) = call(
        late_kernel,
        [jax.ShapeDtypeStruct((ROWS_DEV, width), jnp.bfloat16)],
        [VMEM] * 7,
        [pltpu.VMEM((4 * PIECE, TILE), jnp.bfloat16)] * 2,
        TOKENS * ROWS_DEV * width,
        4 * ROWS_DEV * width,
        (slab, sums, acc, pivot, square, three3, rest3),
    )
    return out


def solution(mesh):
    fine = Mesh(mesh.devices.reshape(4, 4, 2, 8, 2), ALL)
    out_specs = P(("x", "yh"), ("yl", "z", "c"))
    return jax.shard_map(per_device, mesh=fine, in_specs=(P(ALL, None),), out_specs=out_specs, check_vma=False)
```

```python
import jax
import jax.numpy as jnp
import numpy as np
from jax import lax
from jax.experimental import pallas as pl
from jax.experimental.pallas import tpu as pltpu
from jax.sharding import Mesh, PartitionSpec as P

ROWS_DEV = 512
EPS = 1e-06
TOKENS = 2048
FIRST = 1408
PIECE = 128
TILE = 256
ALL = ("x", "yh", "yl", "z", "c")

SLOTS = [(0, 0), (1, 0), (2, 0), (3, 0), (0, 1), (1, 1), (0, 2), (1, 2), (0, 3), (1, 3)]
SLOTS += [(2, 1), (3, 1), (2, 2), (3, 2), (2, 3), (3, 3)]


def exchange(values, axis, step):
    perm = []
    for i in range(4):
        for core in range(2):
            flip = 1 if core == step else 3
            perm.append((i * 2 + core, (i ^ flip) * 2 + core))
    return lax.ppermute(values, (axis, "c"), perm)


def swap_places(values):
    perm = [(a * 32 + y * 16 + b, b * 32 + y * 16 + a) for a in range(16) for y in range(2) for b in range(16)]
    return lax.ppermute(values, ALL, perm)


EVEN = [1, 0, 3, 2, 5, 4, 7, 6]
ODD = [7, 2, 1, 4, 3, 6, 5, 0]
Z_STEPS = [([3, 6, 5, 0, 7, 2, 1, 4], [5, 4, 7, 6, 1, 0, 3, 2]), (ODD, EVEN), (EVEN, ODD)]


def z_permute(values, step):
    perm = [(z * 2 + core, Z_STEPS[step][core][z] * 2 + core) for z in range(8) for core in range(2)]
    return lax.ppermute(values, ("z", "c"), perm)


def z_places():
    held = {(z, core): [z] for z in range(8) for core in range(2)}
    for step in range(3):
        held = {(z, core): held[z, core] + held[Z_STEPS[step][core][z], core] for z, core in held}
    return np.array([[np.argsort(held[z, core]) for core in range(2)] for z in range(8)], np.int32)


def fold(values):
    return jnp.sum(values.reshape(values.shape[0] // 8, 8, values.shape[1]), axis=0)


def slab_kernel(place_ref, mine2_ref, mine3_ref, other2_ref, other3_ref, out_ref, sums_ref, whole):
    n = TOKENS // PIECE
    for first in range(0, ROWS_DEV, TILE):
        lanes = slice(first, first + TILE)
        total = jnp.zeros((8, TILE), jnp.float32)
        for part, ref in enumerate((mine2_ref, mine3_ref, other2_ref, other3_ref)):

            def add(i, total, part=part, ref=ref):
                start = pl.multiple_of(i * PIECE, PIECE)
                values = ref[pl.ds(start, PIECE), lanes]
                whole[pl.ds(start + part * (TOKENS // 4), PIECE), lanes] = values
                return total + fold(values.astype(jnp.float32))

            total = lax.fori_loop(0, n // 4, add, total)
        mean = jnp.sum(total, axis=0, keepdims=True) / TOKENS

        def rows(i):
            return whole[pl.ds(pl.multiple_of(i * PIECE, PIECE), PIECE), lanes].astype(jnp.float32)

        def square(i, total):
            centered = rows(i) - mean
            return total + fold(centered * centered)

        variance = jnp.sum(lax.fori_loop(0, n, square, jnp.zeros((8, TILE), jnp.float32)), axis=0, keepdims=True) / TOKENS
        scale = 1.0 / jnp.sqrt(variance + EPS)
        sums = jnp.zeros((TILE, 1), jnp.float32)
        for slot in range(n):
            standard = ((rows(place_ref[slot]) - mean) * scale).T.astype(jnp.bfloat16)
            out_ref[first : first + TILE, slot * PIECE : (slot + 1) * PIECE] = standard
            sums += jnp.sum(standard.astype(jnp.float32), axis=1, keepdims=True)
        sums_ref[first : first + TILE, :] = jnp.broadcast_to(sums, (TILE, 128))


def call(kernel, outs, in_specs, scratch, flops, moved, args):
    return pl.pallas_call(
        kernel,
        out_shape=outs,
        in_specs=in_specs,
        out_specs=[pl.BlockSpec(memory_space=pltpu.VMEM)] * len(outs),
        scratch_shapes=scratch,
        compiler_params=pltpu.CompilerParams(vmem_limit_bytes=32 * 2**20),
        cost_estimate=pl.CostEstimate(flops=flops // 64, bytes_accessed=moved // 64, transcendentals=0),
    )(*args)


VMEM = pl.BlockSpec(memory_space=pltpu.VMEM)


def slab_standard(quarters, place):
    return call(
        slab_kernel,
        [jax.ShapeDtypeStruct((ROWS_DEV, TOKENS), jnp.bfloat16), jax.ShapeDtypeStruct((ROWS_DEV, 128), jnp.float32)],
        [pl.BlockSpec(memory_space=pltpu.SMEM)] + [VMEM] * 4,
        [pltpu.VMEM((TOKENS, ROWS_DEV), jnp.bfloat16)],
        8 * TOKENS * ROWS_DEV,
        4 * TOKENS * ROWS_DEV,
        (place, *quarters),
    )


def tile_at(ref, part, lanes):
    return ref[pl.ds(pl.multiple_of(part * PIECE, PIECE), PIECE), lanes].astype(jnp.float32)


def over_tiles(width, scratch, body):
    pairs = width // (2 * TILE)

    @pl.loop(0, pairs)
    def _(j):
        for i in range(2):
            body((2 * j + i) * TILE, TILE, scratch[i])

    for i, start in enumerate(range(pairs * 2 * TILE, width, TILE)):
        body(start, min(TILE, width - start), scratch[i])


def at(start, size):
    return pl.ds(pl.multiple_of(start, 128), size)


def product(slab_ref, shifted, spans, size):
    acc, row = None, 0
    for first, depth in spans:
        part = jnp.dot(
            slab_ref[:, first : first + depth], shifted[row : row + depth, :size], preferred_element_type=jnp.float32
        )
        acc = part if acc is None else acc + part
        row += depth
    return acc


def early_kernel(slab_ref, own, x1, x2, y1, y2, x3, y3, acc_ref, pivot_ref, square_ref, *scratch):
    width = own.shape[1]

    def tiles(pieces, offset, columns, spans):
        def body(start, size, shifted):
            lanes = at(start + offset, size)

            def load(piece):
                ref, part, whole = piece
                return tile_at(ref, part, lanes if whole else at(start, size))

            total = jnp.zeros((8, size), jnp.float32)
            for piece in pieces:
                total += fold(load(piece))
            pivot = jnp.sum(total, axis=0, keepdims=True) / (len(pieces) * PIECE)
            square = jnp.zeros((8, size), jnp.float32)
            for i, piece in enumerate(pieces):
                values = load(piece) - pivot
                square += fold(values * values)
                shifted[i * PIECE : (i + 1) * PIECE, :size] = values.astype(jnp.bfloat16)
            pivot_ref[:, lanes] = jnp.broadcast_to(pivot, (8, size))
            square_ref[:, lanes] = square
            acc_ref[:, lanes] = product(slab_ref, shifted, spans, size)

        over_tiles(columns, scratch, body)

    near = [(own, 0, True), (x1, 0, True), (x2, 0, True), (x2, 1, True)]
    tiles(
        near
        + [(y1, 0, False), (x3, 0, False), (y2, 0, False), (x3, 1, False), (y2, 1, False), (x3, 2, False)],
        0,
        FIRST,
        [(0, 1280)],
    )
    tiles(near + [(y3, i, False) for i in range(4)], FIRST, width - FIRST, [(0, 768), (1280, 256)])


def late_kernel(slab_ref, sums_ref, acc_ref, pivot_ref, square_ref, far, opposite, y4, out_ref, *scratch):
    width = acc_ref.shape[1]

    def tiles(pieces, offset, columns, spans):
        def body(start, size, shifted):
            lanes = at(start + offset, size)
            pivot = pivot_ref[0:1, lanes]
            total = jnp.zeros((8, size), jnp.float32)
            square = square_ref[:, lanes]
            for i, (ref, part) in enumerate(pieces):
                values = tile_at(ref, part, at(start, size)) - pivot
                total += fold(values)
                square += fold(values * values)
                shifted[i * PIECE : (i + 1) * PIECE, :size] = values.astype(jnp.bfloat16)
            delta = jnp.sum(total, axis=0, keepdims=True) / TOKENS
            variance = jnp.sum(square, axis=0, keepdims=True) / TOKENS - delta * delta
            scale = 1.0 / (jnp.sqrt(jnp.maximum(variance, 0.0) + EPS) * TOKENS)
            acc = acc_ref[:, lanes] + product(slab_ref, shifted, spans, size)
            out_ref[:, lanes] = ((acc - sums_ref[:, 0:1] * delta) * scale).astype(jnp.bfloat16)

        over_tiles(columns, scratch, body)

    tiles([(ref, i) for i in range(3) for ref in (far, opposite)], 0, FIRST, [(1280, 768)])
    tiles([(y4, i) for i in (0, 1, 4, 5, 2, 3, 6, 7)], FIRST, width - FIRST, [(768, 512), (1536, 512)])


def per_device(activations):
    together = lax.optimization_barrier
    tok, units = activations.shape
    n_col = 32
    width = units // n_col
    slab = activations[:, : 16 * ROWS_DEV].reshape(tok, 1, 16, ROWS_DEV)
    with_slab = jnp.concatenate(
        [activations.reshape(tok, 2, 16, width), jnp.broadcast_to(slab, (tok, 2, 16, ROWS_DEV))], axis=3
    )
    block = lax.all_to_all(
        with_slab.reshape(tok, n_col * (width + ROWS_DEV)), ("yl", "z", "c"), split_axis=1, concat_axis=0, tiled=True
    )
    own, own_first, slab0 = block[:, :width], block[:, :FIRST], block[:, width:]
    y1 = exchange(own_first, "yh", 0)
    x1 = exchange(own, "x", 0)
    slab0 = swap_places(slab0)
    x1, y1, slab0 = together((x1, y1, slab0))
    y2 = exchange(jnp.concatenate([own_first, y1], axis=0), "yh", 1)
    x2 = exchange(jnp.concatenate([own, x1], axis=0), "x", 1)
    slab1 = jnp.concatenate([slab0, z_permute(slab0, 0)], axis=0)
    slab2 = z_permute(slab1, 1)
    rest = jnp.concatenate([own[:, FIRST:], x1[:, FIRST:], x2[:, FIRST:]], axis=0)
    x2, y2, rest, slab1, slab2 = together((x2, y2, rest, slab1, slab2))
    three = jnp.concatenate([y1, y2], axis=0)
    y3 = exchange(rest, "yh", 0)
    x3 = exchange(three, "x", 0)
    slab2 = jnp.concatenate([slab1, slab2], axis=0)
    slab3 = z_permute(slab2, 2)
    x3, y3, slab2, slab3 = together((x3, y3, slab2, slab3))
    rest = jnp.concatenate([rest, y3], axis=0)
    y4 = exchange(rest, "yh", 1)
    x4 = [exchange(part, "x", 1) for part in (three, x3)]

    quarters = [slab2, slab3] + [lax.ppermute(part, "c", [(0, 1), (1, 0)]) for part in (slab2, slab3)]

    near = jnp.where(lax.axis_index("c") == 0, 1, 3)
    flips = [0, near, 4 - near, 2]
    token_of = jnp.stack(
        [(lax.axis_index("x") ^ flips[i]) * 4 + (lax.axis_index("yh") ^ flips[j]) for i, j in SLOTS]
    )
    core = lax.axis_index("c")
    table = jnp.asarray(z_places())[lax.axis_index("z")]
    table = jnp.where(core == 0, table, table[::-1])
    place = jnp.where(token_of % 2 == core, table[0][token_of // 2], table[1][token_of // 2] + 8)
    slab, sums = slab_standard(quarters, place.astype(jnp.int32))

    wide = jax.ShapeDtypeStruct((8, width), jnp.float32)
    acc, pivot, square = call(
        early_kernel,
        [jax.ShapeDtypeStruct((ROWS_DEV, width), jnp.float32), wide, wide],
        [VMEM] * 8,
        [pltpu.VMEM((1280, TILE), jnp.bfloat16)] * 2,
        TOKENS * ROWS_DEV * width,
        4 * ROWS_DEV * width,
        (slab, own, x1, x2, y1, y2, x3, y3),
    )
    (out,) = call(
        late_kernel,
        [jax.ShapeDtypeStruct((ROWS_DEV, width), jnp.bfloat16)],
        [VMEM] * 8,
        [pltpu.VMEM((1024, TILE), jnp.bfloat16)] * 2,
        TOKENS * ROWS_DEV * width,
        4 * ROWS_DEV * width,
        (slab, sums, acc, pivot, square, *x4, y4),
    )
    return out


def solution(mesh):
    fine = Mesh(mesh.devices.reshape(4, 4, 2, 8, 2), ALL)
    out_specs = P(("x", "yh"), ("yl", "z", "c"))
    return jax.shard_map(per_device, mesh=fine, in_specs=(P(ALL, None),), out_specs=out_specs, check_vma=False)
```

```python
import jax
import jax.numpy as jnp
import numpy as np
from jax import lax
from jax.experimental import pallas as pl
from jax.experimental.pallas import tpu as pltpu
from jax.sharding import Mesh, PartitionSpec as P

ROWS_DEV = 512
EPS = 1e-06
TOKENS = 2048
FIRST = 1408
PIECE = 128
TILE = 256
ALL = ("x", "yh", "yl", "z", "c")

SLOTS = [(0, 0), (1, 0), (2, 0), (3, 0), (0, 1), (1, 1), (0, 2), (1, 2), (0, 3), (1, 3)]
SLOTS += [(2, 1), (3, 1), (2, 2), (3, 2), (2, 3), (3, 3)]


def exchange(values, axis, step):
    perm = []
    for i in range(4):
        for core in range(2):
            flip = 1 if core == step else 3
            perm.append((i * 2 + core, (i ^ flip) * 2 + core))
    return lax.ppermute(values, (axis, "c"), perm)


def swap_places(values):
    perm = [(a * 32 + y * 16 + b, b * 32 + y * 16 + a) for a in range(16) for y in range(2) for b in range(16)]
    return lax.ppermute(values, ALL, perm)


EVEN = [1, 0, 3, 2, 5, 4, 7, 6]
ODD = [7, 2, 1, 4, 3, 6, 5, 0]
Z_STEPS = [([3, 6, 5, 0, 7, 2, 1, 4], [5, 4, 7, 6, 1, 0, 3, 2]), (ODD, EVEN), (EVEN, ODD)]


def z_permute(values, step):
    perm = [(z * 2 + core, Z_STEPS[step][core][z] * 2 + core) for z in range(8) for core in range(2)]
    return lax.ppermute(values, ("z", "c"), perm)


def z_places():
    held = {(z, core): [z] for z in range(8) for core in range(2)}
    for step in range(3):
        held = {(z, core): held[z, core] + held[Z_STEPS[step][core][z], core] for z, core in held}
    return np.array([[np.argsort(held[z, core]) for core in range(2)] for z in range(8)], np.int32)


def fold(values):
    return jnp.sum(values.reshape(values.shape[0] // 8, 8, values.shape[1]), axis=0)


def slab_kernel(place_ref, mine2_ref, mine3_ref, other2_ref, other3_ref, out_ref, sums_ref, whole):
    n = TOKENS // PIECE
    for first in range(0, ROWS_DEV, TILE):
        lanes = slice(first, first + TILE)
        total = jnp.zeros((8, TILE), jnp.float32)
        for part, ref in enumerate((mine2_ref, mine3_ref, other2_ref, other3_ref)):

            def add(i, total, part=part, ref=ref):
                start = pl.multiple_of(i * PIECE, PIECE)
                values = ref[pl.ds(start, PIECE), lanes]
                whole[pl.ds(start + part * (TOKENS // 4), PIECE), lanes] = values
                return total + fold(values.astype(jnp.float32))

            total = lax.fori_loop(0, n // 4, add, total)
        mean = jnp.sum(total, axis=0, keepdims=True) / TOKENS

        def rows(i):
            return whole[pl.ds(pl.multiple_of(i * PIECE, PIECE), PIECE), lanes].astype(jnp.float32)

        def square(i, total):
            centered = rows(i) - mean
            return total + fold(centered * centered)

        variance = jnp.sum(lax.fori_loop(0, n, square, jnp.zeros((8, TILE), jnp.float32)), axis=0, keepdims=True) / TOKENS
        scale = 1.0 / jnp.sqrt(variance + EPS)
        sums = jnp.zeros((TILE, 1), jnp.float32)
        for slot in range(n):
            standard = ((rows(place_ref[slot]) - mean) * scale).T.astype(jnp.bfloat16)
            out_ref[first : first + TILE, slot * PIECE : (slot + 1) * PIECE] = standard
            sums += jnp.sum(standard.astype(jnp.float32), axis=1, keepdims=True)
        sums_ref[first : first + TILE, :] = jnp.broadcast_to(sums, (TILE, 128))


def call(kernel, outs, in_specs, scratch, flops, moved, args):
    return pl.pallas_call(
        kernel,
        out_shape=outs,
        in_specs=in_specs,
        out_specs=[pl.BlockSpec(memory_space=pltpu.VMEM)] * len(outs),
        scratch_shapes=scratch,
        compiler_params=pltpu.CompilerParams(vmem_limit_bytes=32 * 2**20),
        cost_estimate=pl.CostEstimate(flops=flops // 64, bytes_accessed=moved // 64, transcendentals=0),
    )(*args)


VMEM = pl.BlockSpec(memory_space=pltpu.VMEM)


def slab_standard(quarters, place):
    return call(
        slab_kernel,
        [jax.ShapeDtypeStruct((ROWS_DEV, TOKENS), jnp.bfloat16), jax.ShapeDtypeStruct((ROWS_DEV, 128), jnp.float32)],
        [pl.BlockSpec(memory_space=pltpu.SMEM)] + [VMEM] * 4,
        [pltpu.VMEM((TOKENS, ROWS_DEV), jnp.bfloat16)],
        8 * TOKENS * ROWS_DEV,
        4 * TOKENS * ROWS_DEV,
        (place, *quarters),
    )


def tile_at(ref, part, lanes):
    return ref[pl.ds(pl.multiple_of(part * PIECE, PIECE), PIECE), lanes].astype(jnp.float32)


def over_tiles(width, scratch, body):
    pairs = width // (2 * TILE)

    @pl.loop(0, pairs)
    def _(j):
        for i in range(2):
            body((2 * j + i) * TILE, TILE, scratch[i])

    for i, start in enumerate(range(pairs * 2 * TILE, width, TILE)):
        body(start, min(TILE, width - start), scratch[i])


def at(start, size):
    return pl.ds(pl.multiple_of(start, 128), size)


def product(slab_ref, shifted, spans, size):
    acc, row = None, 0
    for first, depth in spans:
        part = jnp.dot(
            slab_ref[:, first : first + depth], shifted[row : row + depth, :size], preferred_element_type=jnp.float32
        )
        acc = part if acc is None else acc + part
        row += depth
    return acc


def early_kernel(slab_ref, own, x1, x2, y1, y2, x3, y3, acc_ref, pivot_ref, square_ref, *scratch):
    width = own.shape[1]

    def tiles(pieces, offset, columns, spans):
        def body(start, size, shifted):
            lanes = at(start + offset, size)

            def load(piece):
                ref, part, whole = piece
                return tile_at(ref, part, lanes if whole else at(start, size))

            total = jnp.zeros((8, size), jnp.float32)
            for piece in pieces:
                total += fold(load(piece))
            pivot = jnp.sum(total, axis=0, keepdims=True) / (len(pieces) * PIECE)
            square = jnp.zeros((8, size), jnp.float32)
            for i, piece in enumerate(pieces):
                values = load(piece) - pivot
                square += fold(values * values)
                shifted[i * PIECE : (i + 1) * PIECE, :size] = values.astype(jnp.bfloat16)
            pivot_ref[:, lanes] = jnp.broadcast_to(pivot, (8, size))
            square_ref[:, lanes] = square
            acc_ref[:, lanes] = product(slab_ref, shifted, spans, size)

        over_tiles(columns, scratch, body)

    near = [(own, 0, True), (x1, 0, True), (x2, 0, True), (x2, 1, True)]
    tiles(
        near
        + [(y1, 0, False), (x3, 0, False), (y2, 0, False), (x3, 1, False), (y2, 1, False), (x3, 2, False)],
        0,
        FIRST,
        [(0, 1280)],
    )
    tiles(near + [(y3, i, False) for i in range(4)], FIRST, width - FIRST, [(0, 768), (1280, 256)])


def late_kernel(slab_ref, sums_ref, acc_ref, pivot_ref, square_ref, x4, y4, out_ref, *scratch):
    width = acc_ref.shape[1]

    def tiles(pieces, offset, columns, spans):
        def body(start, size, shifted):
            lanes = at(start + offset, size)
            pivot = pivot_ref[0:1, lanes]
            total = jnp.zeros((8, size), jnp.float32)
            square = square_ref[:, lanes]
            for i, (ref, part) in enumerate(pieces):
                values = tile_at(ref, part, at(start, size)) - pivot
                total += fold(values)
                square += fold(values * values)
                shifted[i * PIECE : (i + 1) * PIECE, :size] = values.astype(jnp.bfloat16)
            delta = jnp.sum(total, axis=0, keepdims=True) / TOKENS
            variance = jnp.sum(square, axis=0, keepdims=True) / TOKENS - delta * delta
            scale = 1.0 / (jnp.sqrt(jnp.maximum(variance, 0.0) + EPS) * TOKENS)
            acc = acc_ref[:, lanes] + product(slab_ref, shifted, spans, size)
            out_ref[:, lanes] = ((acc - sums_ref[:, 0:1] * delta) * scale).astype(jnp.bfloat16)

        over_tiles(columns, scratch, body)

    tiles([(x4, i) for i in (0, 3, 1, 4, 2, 5)], 0, FIRST, [(1280, 768)])
    tiles([(y4, i) for i in (0, 1, 4, 5, 2, 3, 6, 7)], FIRST, width - FIRST, [(768, 512), (1536, 512)])


def per_device(activations):
    together = lax.optimization_barrier
    tok, units = activations.shape
    n_col = 32
    width = units // n_col
    slab = activations[:, : 16 * ROWS_DEV].reshape(tok, 1, 16, ROWS_DEV)
    with_slab = jnp.concatenate(
        [activations.reshape(tok, 2, 16, width), jnp.broadcast_to(slab, (tok, 2, 16, ROWS_DEV))], axis=3
    )
    block = lax.all_to_all(
        with_slab.reshape(tok, n_col * (width + ROWS_DEV)), ("yl", "z", "c"), split_axis=1, concat_axis=0, tiled=True
    )
    own, own_first, slab0 = block[:, :width], block[:, :FIRST], block[:, width:]
    y1 = exchange(own_first, "yh", 0)
    x1 = exchange(own, "x", 0)
    slab0 = swap_places(slab0)
    x1, y1, slab0 = together((x1, y1, slab0))
    y2 = exchange(jnp.concatenate([own_first, y1], axis=0), "yh", 1)
    x2 = exchange(jnp.concatenate([own, x1], axis=0), "x", 1)
    slab1 = jnp.concatenate([slab0, z_permute(slab0, 0)], axis=0)
    slab2 = z_permute(slab1, 1)
    rest = jnp.concatenate([own[:, FIRST:], x1[:, FIRST:], x2[:, FIRST:]], axis=0)
    x2, y2, rest, slab1 = together((x2, y2, rest, slab1))
    three = jnp.concatenate([y1, y2], axis=0)
    y3 = exchange(rest, "yh", 0)
    x3 = exchange(three, "x", 0)
    slab2 = jnp.concatenate([slab1, slab2], axis=0)
    slab3 = z_permute(slab2, 2)
    x3, y3, slab2, slab3 = together((x3, y3, slab2, slab3))
    rest = jnp.concatenate([rest, y3], axis=0)
    y4 = exchange(rest, "yh", 1)
    x4 = exchange(jnp.concatenate([three, x3], axis=0), "x", 1)

    quarters = [slab2, slab3] + [lax.ppermute(part, "c", [(0, 1), (1, 0)]) for part in (slab2, slab3)]

    near = jnp.where(lax.axis_index("c") == 0, 1, 3)
    flips = [0, near, 4 - near, 2]
    token_of = jnp.stack(
        [(lax.axis_index("x") ^ flips[i]) * 4 + (lax.axis_index("yh") ^ flips[j]) for i, j in SLOTS]
    )
    core = lax.axis_index("c")
    table = jnp.asarray(z_places())[lax.axis_index("z")]
    table = jnp.where(core == 0, table, table[::-1])
    place = jnp.where(token_of % 2 == core, table[0][token_of // 2], table[1][token_of // 2] + 8)
    slab, sums = slab_standard(quarters, place.astype(jnp.int32))

    wide = jax.ShapeDtypeStruct((8, width), jnp.float32)
    acc, pivot, square = call(
        early_kernel,
        [jax.ShapeDtypeStruct((ROWS_DEV, width), jnp.float32), wide, wide],
        [VMEM] * 8,
        [pltpu.VMEM((1280, TILE), jnp.bfloat16)] * 2,
        TOKENS * ROWS_DEV * width,
        4 * ROWS_DEV * width,
        (slab, own, x1, x2, y1, y2, x3, y3),
    )
    (out,) = call(
        late_kernel,
        [jax.ShapeDtypeStruct((ROWS_DEV, width), jnp.bfloat16)],
        [VMEM] * 7,
        [pltpu.VMEM((1024, TILE), jnp.bfloat16)] * 2,
        TOKENS * ROWS_DEV * width,
        4 * ROWS_DEV * width,
        (slab, sums, acc, pivot, square, x4, y4),
    )
    return out


def solution(mesh):
    fine = Mesh(mesh.devices.reshape(4, 4, 2, 8, 2), ALL)
    out_specs = P(("x", "yh"), ("yl", "z", "c"))
    return jax.shard_map(per_device, mesh=fine, in_specs=(P(ALL, None),), out_specs=out_specs, check_vma=False)
```
